512 devices in a mesh: seq: 64 (over y, z), head: 8 (over x, core).
Axes of the slice: x: 4, y: 4, z: 16, core: 2. Of those that a mesh axis runs over, the one named last changes fastest.
Arguments:
- queries: bfloat16 [32768, 4096], P('seq', 'head'), may hold values from -6 to 6
- keys: bfloat16 [32768, 4096], P('seq', 'head'), may hold values from -6 to 6
- values: bfloat16 [32768, 4096], P('seq', 'head'), may hold values from -6 to 6
- out_weight: bfloat16 [4096, 4096], P('head', 'seq'), may hold values from -0.09375 to 0.09375
- head_gain: float32 [4096], P('head'), may hold values from 0.1 to 1.9
Outputs:
- layer_out: bfloat16 [32768, 4096], P(('seq', 'head'))
The draws below stay inside these ranges and needn't reach their ends.
All inputs are finite; a program needn't handle non-finite values.
Results may differ from the reference program's by a relative error of at most 0.017.
Values may be sent and summed in bfloat16 or wider, within the bound.
No kernel may reach another device: no remote copies, remote signals or barrier semaphores. Data moves between devices by JAX's collectives and lax.ppermute only.
A program may use at most 64 MiB of HBM per device.

```python
import jax
import jax.numpy as jnp
from jax import lax

H = 32
DH = 128
D = 4096
TOK_DEV = 512
HD = 4096
TOKENS = 32768
N_HEAD = 8


def steps_of(own_key, extent, split, low, top_value):
    def one(axis_at, blocks):
        steps = jax.random.uniform(jax.random.fold_in(jax.random.fold_in(own_key, 6), axis_at), (blocks,), jnp.float32, low / len(split), top_value / len(split))
        return jnp.repeat(jnp.exp(steps), extent[axis_at] // blocks).reshape((-1,) + (1,) * (len(extent) - axis_at - 1))

    gain = one(*split[0])
    for cut in split[1:]:
        gain = gain * one(*cut)
    return gain


def noise(rng, dims, width, bound, pieces=(), kind=jnp.bfloat16):
    level = steps_of(rng, dims, pieces, -0.22, 0.18) if pieces else 1.0
    drawn = jax.random.normal(rng, dims, jnp.float32) * width * level
    return jnp.minimum(jnp.maximum(drawn, -bound), bound).astype(kind)


def setup_inputs(seed: int = 0) -> dict:
    splits = jax.random.split(jax.random.key(seed), 6)
    queries = noise(splits[0], (TOKENS, HD), 1.0, 6.0, ((0, 64), (1, 8)))
    keys = noise(splits[1], (TOKENS, HD), 1.0, 6.0, ((0, 64), (1, 8)))
    values = noise(splits[2], (TOKENS, HD), 1.0, 6.0, ((0, 64), (1, 8)))
    out_weight = noise(splits[3], (HD, D), HD ** -0.5, 0.09375, ((0, 8), (1, 64)))
    head_gain = jnp.clip(1.0 + 0.18 * jax.random.normal(splits[4], (HD,), jnp.float32), 0.1, 1.9)
    return {"queries": queries, "keys": keys, "values": values, "out_weight": out_weight, "head_gain": head_gain}


def feature(inputs):
    return jax.nn.elu(inputs.astype(jnp.float32)) + 1.0

def reference(queries, keys, values, out_weight, head_gain):
    highest = lax.Precision.HIGHEST
    token_total = queries.shape[0]
    block_count = token_total // TOK_DEV
    query_bf = feature(queries).astype(jnp.bfloat16)
    key_bf = feature(keys).astype(jnp.bfloat16)
    query_feat = lax.optimization_barrier(query_bf).astype(jnp.float32).reshape(block_count, TOK_DEV, H, DH)
    key_feat = lax.optimization_barrier(key_bf).astype(jnp.float32).reshape(block_count, TOK_DEV, H, DH)
    value_feat = values.astype(jnp.float32).reshape(block_count, TOK_DEV, H, DH)
    causal = jnp.tril(jnp.ones((TOK_DEV, TOK_DEV), dtype=bool))
    gain_heads = head_gain.reshape(H, DH)

    def advance(memory, inputs):
        block_query, block_key, block_value = inputs
        numerator = jnp.einsum('thd,hde->the', block_query, memory, precision=highest)
        scores = jnp.einsum('thd,shd->hts', block_query, block_key, precision=highest)
        scores = jnp.where(causal[None, :, :], scores, 0.0)
        weights_bf = scores.astype(jnp.bfloat16)
        weights = lax.optimization_barrier(weights_bf).astype(jnp.float32)
        attended = numerator + jnp.einsum('hts,she->the', weights, block_value, precision=highest)
        mean_square = lax.optimization_barrier(jnp.mean(attended * attended, axis=-1, keepdims=True))
        normed = (attended * lax.rsqrt(mean_square + 1e-05) * gain_heads[None]).astype(jnp.bfloat16)
        memory = memory + jnp.einsum('thd,the->hde', block_key, block_value, precision=highest)
        return (memory, normed)
    start_memory = jnp.zeros((H, DH, DH), jnp.float32)
    final_memory, normed_all = lax.scan(advance, start_memory, (query_feat, key_feat, value_feat))
    normed_all = normed_all.reshape(token_total, H * DH)
    group_width = H * DH // N_HEAD
    summed = jnp.zeros((token_total, D), jnp.float32)
    for group_index in range(N_HEAD):
        columns = normed_all[:, group_index * group_width:(group_index + 1) * group_width]
        weight_rows = out_weight[group_index * group_width:(group_index + 1) * group_width, :]
        partial_bf = jnp.dot(columns, weight_rows, preferred_element_type=jnp.float32).astype(jnp.bfloat16)
        summed = summed + lax.optimization_barrier(partial_bf).astype(jnp.float32)
    return summed.astype(jnp.bfloat16)
```

```python
import functools

import jax
import jax.numpy as jnp
from jax import lax
from jax.experimental import pallas as pl
from jax.experimental.pallas import tpu as pltpu
from jax.sharding import PartitionSpec as P

DH = 128
NY, NZ = 4, 16
Y_GROUPS = [[y * NZ + z for y in range(NY)] for z in range(NZ)]
Z_GROUPS = [[y * NZ + z for z in range(NZ)] for y in range(NY)]


def feature(inputs):
    return jax.nn.elu(inputs.astype(jnp.float32)) + 1.0


def prior_of(memory):
    count = lax.axis_size("seq")
    shape = memory.shape
    pieces = memory.astype(jnp.bfloat16).reshape(-1, DH)
    pieces = lax.all_to_all(pieces, "seq", 0, 0, tiled=True)
    earlier = jnp.tril(jnp.ones((count, count), jnp.bfloat16), -1)
    sums = jnp.dot(earlier, pieces.reshape(count, -1), preferred_element_type=jnp.float32)
    sums = sums.astype(jnp.bfloat16).reshape(-1, DH)
    return lax.all_to_all(sums, "seq", 0, 0, tiled=True).reshape(shape)


def project_kernel(normed_ref, weight_ref, out_ref):
    zs, _, cols, depth = weight_ref.shape
    weight = weight_ref[...].reshape(zs * cols, depth)
    out_ref[...] = lax.dot_general(
        normed_ref[...], weight, (((1,), (1,)), ((), ())), preferred_element_type=jnp.float32
    ).astype(out_ref.dtype)


def project(normed, weight):
    rows, depth = normed.shape
    _, _, cols, _ = weight.shape
    zs = 8
    return pl.pallas_call(
        project_kernel,
        grid=(NY, NZ // zs),
        in_specs=[
            pl.BlockSpec((rows, depth), lambda y, z: (0, 0)),
            pl.BlockSpec((zs, 1, cols, depth), lambda y, z: (z, y, 0, 0)),
        ],
        out_specs=pl.BlockSpec((rows, zs * cols), lambda y, z: (0, y * (NZ // zs) + z)),
        out_shape=jax.ShapeDtypeStruct((rows, NY * NZ * cols), jnp.bfloat16),
        compiler_params=pltpu.CompilerParams(vmem_limit_bytes=32 * 1024 * 1024),
        cost_estimate=pl.CostEstimate(
            flops=2 * rows * depth * NY * NZ * cols, bytes_accessed=9 << 20, transcendentals=0
        ),
    )(normed, weight)


def body(queries, keys, values, out_weight, head_gain):
    row_count = queries.shape[0]
    local_heads = queries.shape[1] // DH
    weight_t = lax.all_gather(out_weight.T, "seq", axis=0, tiled=True, axis_index_groups=Y_GROUPS)
    weight_t, keys, values = lax.optimization_barrier((weight_t, keys, values))
    weight_t = lax.all_gather(weight_t, "seq", axis=0, tiled=True, axis_index_groups=Z_GROUPS)
    query_bf = feature(queries).astype(jnp.bfloat16).reshape(row_count, local_heads, DH)
    key_bf = feature(keys).astype(jnp.bfloat16).reshape(row_count, local_heads, DH)
    value_bf = values.reshape(row_count, local_heads, DH)
    memory = jnp.einsum("thd,the->hde", key_bf, value_bf, preferred_element_type=jnp.float32)
    prior = prior_of(memory)
    numerator = jnp.einsum("thd,hde->the", query_bf, prior, preferred_element_type=jnp.float32)
    causal = jnp.tril(jnp.ones((row_count, row_count), dtype=bool))
    scores = jnp.einsum("thd,shd->hts", query_bf, key_bf, preferred_element_type=jnp.float32)
    scores = jnp.where(causal[None, :, :], scores, 0.0)
    weights = scores.astype(jnp.bfloat16)
    attended = numerator + jnp.einsum(
        "hts,she->the", weights, value_bf, preferred_element_type=jnp.float32
    )
    mean_square = jnp.mean(attended * attended, axis=-1, keepdims=True)
    gain_heads = head_gain.reshape(local_heads, DH)
    normed = (attended * lax.rsqrt(mean_square + 1e-05) * gain_heads[None]).astype(jnp.bfloat16)
    normed = normed.reshape(row_count, local_heads * DH)
    partial = project(normed, weight_t.reshape(NZ, NY, -1, weight_t.shape[-1]))
    return lax.psum_scatter(partial, "head", scatter_dimension=0, tiled=True)


def solution(mesh):
    placed = (P("seq", "head"), P("seq", "head"), P("seq", "head"), P("head", "seq"), P("head"))
    return jax.shard_map(
        body, mesh=mesh, in_specs=placed, out_specs=P(("seq", "head"), None), check_vma=False
    )
```

```python
import jax
import jax.numpy as jnp
from jax import lax
from jax.experimental import pallas as pl
from jax.experimental.pallas import tpu as pltpu
from jax.sharding import PartitionSpec as P

DH = 128
NX, NY, NZ = 4, 4, 16
Z_GROUPS = [[y * NZ + z for z in range(NZ)] for y in range(NY)]
X_GROUPS = [[0, 2, 4, 6], [1, 3, 5, 7]]
CORES = [(i, i ^ 1) for i in range(8)]
VMEM = pl.BlockSpec(memory_space=pltpu.VMEM)
f32, bf16 = jnp.float32, jnp.bfloat16


def call(kernel, outs, flops, *args):
    return pl.pallas_call(
        kernel,
        in_specs=[VMEM] * len(args),
        out_specs=[VMEM] * len(outs),
        out_shape=outs,
        compiler_params=pltpu.CompilerParams(vmem_limit_bytes=16 << 20),
        cost_estimate=pl.CostEstimate(flops=flops, bytes_accessed=4 << 20, transcendentals=1 << 18),
    )(*args)


def placed_call(kernel, out, flops, place, *args):
    return pl.pallas_call(
        kernel,
        in_specs=[pl.BlockSpec(memory_space=pltpu.SMEM)] + [VMEM] * len(args),
        out_specs=VMEM,
        out_shape=out,
        compiler_params=pltpu.CompilerParams(vmem_limit_bytes=16 << 20),
        cost_estimate=pl.CostEstimate(flops=flops, bytes_accessed=4 << 20, transcendentals=0),
    )(place, *args)


def feature(x):
    x = x.astype(f32)
    return jnp.where(x > 0.0, x + 1.0, jnp.exp(jnp.minimum(x, 0.0))).astype(bf16)


def heads(ref):
    return [slice(h * DH, (h + 1) * DH) for h in range(ref.shape[1] // DH)]


def memory_kernel(keys_ref, values_ref, key_ref, memory_ref):
    for cols in heads(keys_ref):
        key = feature(keys_ref[:, cols])
        key_ref[:, cols] = key
        memory_ref[cols, :] = lax.dot_general(
            key, values_ref[:, cols], (((0,), (0,)), ((), ())), preferred_element_type=f32
        ).astype(bf16)


def local_kernel(queries_ref, key_ref, values_ref, query_ref, attended_ref):
    rows = queries_ref.shape[0]
    step = 256
    for cols in heads(queries_ref):
        query_ref[:, cols] = feature(queries_ref[:, cols])
        for top in range(0, rows, step):
            seen = top + step
            scores = lax.dot_general(
                query_ref[top:seen, cols],
                key_ref[:seen, cols],
                (((1,), (1,)), ((), ())),
                preferred_element_type=f32,
            )
            row = top + lax.broadcasted_iota(jnp.int32, scores.shape, 0)
            column = lax.broadcasted_iota(jnp.int32, scores.shape, 1)
            weights = jnp.where(column <= row, scores, 0.0).astype(bf16)
            attended_ref[top:seen, cols] = jnp.dot(
                weights, values_ref[:seen, cols], preferred_element_type=f32
            )


def prior_kernel(pieces_ref, sums_ref):
    total = jnp.zeros(pieces_ref.shape[1:], f32)
    for block in range(pieces_ref.shape[0]):
        sums_ref[block] = total.astype(bf16)
        total = total + pieces_ref[block].astype(f32)


def split_norm_kernel(core_ref, query_ref, prior_ref, attended_ref, gain_ref, normed_ref):
    core = core_ref[0]
    _, chips, rows, _ = normed_ref.shape
    for cols in heads(query_ref):
        attended = attended_ref[:, cols] + jnp.dot(
            query_ref[:, cols], prior_ref[cols, :], preferred_element_type=f32
        )
        mean_square = jnp.mean(attended * attended, axis=-1, keepdims=True)
        normed = (attended * lax.rsqrt(mean_square + 1e-05) * gain_ref[:, cols]).astype(bf16)
        for chip in range(chips):
            for side in range(2):
                top = (2 * chip + side) * rows
                normed_ref[(core + side) % 2, chip, :, cols] = normed[top : top + rows]


def product(y, tokens_ref, weight_ref, side):
    zs, chips, cols, depth = weight_ref.shape
    total = None
    for turn in range(chips):
        tokens = tokens_ref[(y + turn) % chips, side].reshape(-1, depth)
        weight = weight_ref[:, turn].reshape(zs * cols, depth)
        term = lax.dot_general(tokens, weight, (((1,), (1,)), ((), ())), preferred_element_type=f32)
        total = term if total is None else total + term
    return total


def theirs_kernel(place_ref, tokens_ref, weight_ref, out_ref):
    out_ref[...] = product(place_ref[0], tokens_ref, weight_ref, 1).astype(bf16)


def mine_kernel(place_ref, tokens_ref, weight_ref, got_ref, out_ref):
    total = product(place_ref[0], tokens_ref, weight_ref, 0)
    out_ref[...] = (total + got_ref[...].astype(f32)).astype(bf16)


def project(kernel, place, tokens, weight, *more):
    _, _, chips, rows, depth = tokens.shape
    zs, turns, cols, _ = weight.shape
    step = 4
    block = pl.BlockSpec((chips * rows, step * cols), lambda z: (0, z))
    return pl.pallas_call(
        kernel,
        grid=(zs // step,),
        in_specs=[
            pl.BlockSpec(memory_space=pltpu.SMEM),
            pl.BlockSpec(tokens.shape, lambda z: (0,) * tokens.ndim),
            pl.BlockSpec((step, turns, cols, depth), lambda z: (z, 0, 0, 0)),
            *[block for _ in more],
        ],
        out_specs=block,
        out_shape=jax.ShapeDtypeStruct((chips * rows, zs * cols), bf16),
        compiler_params=pltpu.CompilerParams(vmem_limit_bytes=48 << 20),
        cost_estimate=pl.CostEstimate(
            flops=2 * chips * rows * turns * depth * zs * cols, bytes_accessed=7 << 20, transcendentals=0
        ),
    )(place, tokens, weight, *more)


def join_kernel(parts_ref, out_ref):
    chips, _, cols = parts_ref.shape
    for chip in range(chips):
        out_ref[:, chip * cols : (chip + 1) * cols] = parts_ref[chip]


def to_plane(turn):
    pairs = []
    for y in range(NY):
        for z in range(NZ):
            for x in range(NX):
                for core in range(2):
                    source = (y * NZ + z) * 2 * NX + 2 * x + core
                    target = ((x - turn) % NY * NZ + z) * 2 * NX + 2 * y + core
                    pairs.append((source, target))
    return pairs


def body(queries, keys, values, out_weight, head_gain):
    rows, width = queries.shape
    shape = lambda dims, kind: jax.ShapeDtypeStruct(dims, kind)
    blocks = lax.axis_size("seq")
    y = (lax.axis_index("seq").astype(jnp.int32) // NZ).reshape(1)
    core = (lax.axis_index("head").astype(jnp.int32) % 2).reshape(1)

    own = out_weight.T
    planes = [lax.ppermute(own, ("seq", "head"), to_plane(turn)) for turn in range(NX)]
    weight = lax.all_gather(jnp.concatenate(planes), "seq", axis=0, tiled=True, axis_index_groups=Z_GROUPS)

    key, memory = call(memory_kernel, [shape((rows, width), bf16), shape((width, DH), bf16)], 1 << 26, keys, values)
    pieces = lax.all_to_all(memory.reshape(blocks, -1, DH), "seq", 0, 0, tiled=True)
    (sums,) = call(prior_kernel, [shape(pieces.shape, bf16)], 1 << 16, pieces)
    prior = lax.all_to_all(sums, "seq", 0, 0, tiled=True).reshape(width, DH)
    query, attended = call(
        local_kernel, [shape((rows, width), bf16), shape((rows, width), f32)], 1 << 28, queries, key, values
    )
    normed = placed_call(
        split_norm_kernel,
        shape((2, NX, rows // 8, width), bf16),
        1 << 26,
        core,
        query,
        prior,
        attended,
        head_gain.reshape(1, -1),
    )
    copies = jnp.broadcast_to(normed[None], (NX, *normed.shape))
    tokens = lax.all_to_all(copies, "head", 0, 0, tiled=True, axis_index_groups=X_GROUPS)

    weight = weight.reshape(NZ, NX, *own.shape)
    theirs = project(theirs_kernel, y, tokens, weight)
    got = lax.ppermute(theirs, "head", CORES)
    mine = project(mine_kernel, y, tokens, weight, got)
    parts = lax.all_to_all(mine.reshape(NX, rows // 8, -1), "head", 0, 0, tiled=True, axis_index_groups=X_GROUPS)
    (out,) = call(join_kernel, [shape((rows // 8, NX * parts.shape[-1]), bf16)], 1 << 16, parts)
    return out


def solution(mesh):
    placed = (P("seq", "head"), P("seq", "head"), P("seq", "head"), P("head", "seq"), P("head"))
    return jax.shard_map(
        body, mesh=mesh, in_specs=placed, out_specs=P(("seq", "head"), None), check_vma=False
    )
```

```python
import jax
import jax.numpy as jnp
from jax import lax
from jax.experimental import pallas as pl
from jax.experimental.pallas import tpu as pltpu
from jax.sharding import PartitionSpec as P

DH = 128
NX, NY, NZ = 4, 4, 16
NL = 4
X_GROUPS = [[0, 2, 4, 6], [1, 3, 5, 7]]
CORES = [(i, i ^ 1) for i in range(8)]
VMEM = pl.BlockSpec(memory_space=pltpu.VMEM)
f32, bf16 = jnp.float32, jnp.bfloat16


def call(kernel, outs, flops, *args):
    return pl.pallas_call(
        kernel,
        in_specs=[VMEM] * len(args),
        out_specs=[VMEM] * len(outs),
        out_shape=outs,
        compiler_params=pltpu.CompilerParams(vmem_limit_bytes=16 << 20),
        cost_estimate=pl.CostEstimate(flops=flops, bytes_accessed=4 << 20, transcendentals=1 << 18),
    )(*args)


def placed_call(kernel, out, flops, place, *args):
    return pl.pallas_call(
        kernel,
        in_specs=[pl.BlockSpec(memory_space=pltpu.SMEM)] + [VMEM] * len(args),
        out_specs=jax.tree.map(lambda _: VMEM, out),
        out_shape=out,
        compiler_params=pltpu.CompilerParams(vmem_limit_bytes=16 << 20),
        cost_estimate=pl.CostEstimate(flops=flops, bytes_accessed=4 << 20, transcendentals=0),
    )(place, *args)


def feature(x):
    x = x.astype(f32)
    return jnp.where(x > 0.0, x + 1.0, jnp.exp(jnp.minimum(x, 0.0))).astype(bf16)


def heads(ref):
    return [slice(h * DH, (h + 1) * DH) for h in range(ref.shape[1] // DH)]


def memory_kernel(keys_ref, values_ref, key_ref, memory_ref):
    for cols in heads(keys_ref):
        key = feature(keys_ref[:, cols])
        key_ref[:, cols] = key
        memory_ref[cols, :] = lax.dot_general(
            key, values_ref[:, cols], (((0,), (0,)), ((), ())), preferred_element_type=f32
        ).astype(bf16)


def local_kernel(queries_ref, key_ref, values_ref, query_ref, attended_ref):
    rows = queries_ref.shape[0]
    step = 256
    for cols in heads(queries_ref):
        query_ref[:, cols] = feature(queries_ref[:, cols])
        for top in range(0, rows, step):
            seen = top + step
            scores = lax.dot_general(
                query_ref[top:seen, cols],
                key_ref[:seen, cols],
                (((1,), (1,)), ((), ())),
                preferred_element_type=f32,
            )
            row = top + lax.broadcasted_iota(jnp.int32, scores.shape, 0)
            column = lax.broadcasted_iota(jnp.int32, scores.shape, 1)
            weights = jnp.where(column <= row, scores, 0.0).astype(bf16)
            attended_ref[top:seen, cols] = jnp.dot(
                weights, values_ref[:seen, cols], preferred_element_type=f32
            )


def prior_kernel(pieces_ref, sums_ref):
    total = jnp.zeros(pieces_ref.shape[1:], f32)
    for block in range(pieces_ref.shape[0]):
        sums_ref[block] = total.astype(bf16)
        total = total + pieces_ref[block].astype(f32)


def split_norm_kernel(core_ref, query_ref, prior_ref, attended_ref, gain_ref, normed_ref):
    core = core_ref[0]
    _, chips, rows, _ = normed_ref.shape
    for cols in heads(query_ref):
        attended = attended_ref[:, cols] + jnp.dot(
            query_ref[:, cols], prior_ref[cols, :], preferred_element_type=f32
        )
        mean_square = jnp.mean(attended * attended, axis=-1, keepdims=True)
        normed = (attended * lax.rsqrt(mean_square + 1e-05) * gain_ref[:, cols]).astype(bf16)
        for chip in range(chips):
            for side in range(2):
                top = (2 * chip + side) * rows
                normed_ref[(core + side) % 2, chip, :, cols] = normed[top : top + rows]


def stack_kernel(*refs):
    *block_refs, stack_ref = refs
    for index, block_ref in enumerate(block_refs):
        stack_ref[index] = block_ref[...]


def pass_kernel(block_ref, out_ref):
    out_ref[...] = block_ref[...]


def place_kernel(place_ref, *refs):
    *stacks, low_ref, high_ref, arrived = refs
    z = place_ref[0]
    even = 1 - 2 * (z % 2)
    half = NZ // 2
    waits = []
    for stack, shift in zip(stacks, (0, 1, -1, 2 * even)):
        for index, turn in enumerate((0, 1, -1, 2)):
            owner = (z - shift - NL * turn + 2 * NZ) % NZ
            semaphore = arrived.at[len(waits)]
            to_low = pltpu.make_async_copy(stack.at[index], low_ref.at[owner % half], semaphore)
            to_high = pltpu.make_async_copy(stack.at[index], high_ref.at[owner % half], semaphore)
            pl.when(owner < half)(to_low.start)
            pl.when(owner >= half)(to_high.start)
            waits.append(to_low)
    for copy in waits:
        copy.wait()


def placed(z, stacks, cost):
    half = jax.ShapeDtypeStruct((NZ // 2, *stacks[0].shape[1:]), bf16)
    return pl.pallas_call(
        place_kernel,
        in_specs=[pl.BlockSpec(memory_space=pltpu.SMEM)] + [pl.BlockSpec(memory_space=pl.ANY)] * len(stacks),
        out_specs=[VMEM, VMEM],
        out_shape=[half, half],
        scratch_shapes=[pltpu.SemaphoreType.DMA((NZ,))],
        compiler_params=pltpu.CompilerParams(vmem_limit_bytes=56 << 20),
        cost_estimate=pl.CostEstimate(flops=cost, bytes_accessed=2 << 20, transcendentals=0),
    )(z, *stacks)


def columns_of(weights, step=4):
    at = 0
    for weight in weights:
        blocks, cols, depth = weight.shape
        for first in range(0, blocks, step):
            yield weight[first : first + step].reshape(step * cols, depth), slice(at, at + step * cols)
            at += step * cols


def times(tokens, weight):
    return lax.dot_general(tokens, weight, (((1,), (1,)), ((), ())), preferred_element_type=f32)


def features(tokens_ref, chip):
    return tokens_ref[chip % NX].reshape(-1, tokens_ref.shape[-1])


def near_kernel(place_ref, tokens_ref, *refs):
    *halves, total_ref = refs
    y = place_ref[0]
    sources = [features(tokens_ref, y + turn) for turn in (0, NY - 1, 1)]
    for terms in zip(*(columns_of(pair) for pair in zip(halves[::2], halves[1::2]))):
        total_ref[:, terms[0][1]] = sum(times(tokens, weight) for tokens, (weight, _) in zip(sources, terms))


def far_kernel(place_ref, tokens_ref, total_ref, first_ref, second_ref, mine_ref, theirs_ref):
    tokens = features(tokens_ref, place_ref[0] + 2)
    half = mine_ref.shape[0]
    for weight, cols in columns_of([first_ref, second_ref]):
        total = total_ref[:, cols] + times(tokens, weight)
        mine_ref[:, cols] = total[:half]
        theirs_ref[:, cols] = total[half:].astype(bf16)


def add_kernel(mine_ref, got_ref, out_ref):
    out_ref[...] = (mine_ref[...] + got_ref[...].astype(f32)).astype(bf16)


def join_kernel(parts_ref, out_ref):
    chips, _, cols = parts_ref.shape
    for chip in range(chips):
        out_ref[:, chip * cols : (chip + 1) * cols] = parts_ref[chip]


def to_plane(block):
    pairs = []
    for y in range(NY):
        for z in range(NZ):
            for x in range(NX):
                for core in range(2):
                    source = (y * NZ + z) * 2 * NX + 2 * x + core
                    target = (x * NZ + z) * 2 * NX + 2 * y + core
                    pairs.append((source, target))
    return lax.ppermute(block, ("seq", "head"), pairs)


def along_z(block, shift):
    pairs = [(y * NZ + z, y * NZ + (z + shift(z)) % NZ) for y in range(NY) for z in range(NZ)]
    return lax.ppermute(block, "seq", pairs)


def along_y(block, shift):
    pairs = [(y * NZ + z, (y + shift) % NY * NZ + z) for y in range(NY) for z in range(NZ)]
    return lax.ppermute(block, "seq", pairs)


def after(value, *others):
    return lax.optimization_barrier((value, *others))[0]


def body(queries, keys, values, out_weight, head_gain):
    rows, width = queries.shape
    shape = lambda dims, kind: jax.ShapeDtypeStruct(dims, kind)
    blocks = lax.axis_size("seq")
    place = lax.axis_index("seq").astype(jnp.int32)
    y, z = (place // NZ).reshape(1), (place % NZ).reshape(1)
    core = (lax.axis_index("head").astype(jnp.int32) % 2).reshape(1)

    own = to_plane(out_weight.T)
    (own,) = call(pass_kernel, [shape(own.shape, bf16)], 1<<33, own)
    far = [along_z(own, lambda z, s=s: s) for s in (NL, -NL, 2 * NL)]
    key, memory = call(memory_kernel, [shape((rows, width), bf16), shape((width, DH), bf16)], 1 << 26, keys, values)
    pieces = lax.all_to_all(memory.reshape(blocks, -1, DH), "seq", 0, 0, tiled=True)
    (stack,) = call(stack_kernel, [shape((NL, *own.shape), bf16)], 1<<33, own, *far)
    near = [along_z(stack, s) for s in (lambda z: 1, lambda z: -1, lambda z: 2 - 4 * (z % 2))]
    (sums,) = call(prior_kernel, [shape(pieces.shape, bf16)], 1<<33, pieces)
    prior = lax.all_to_all(sums, "seq", 0, 0, tiled=True).reshape(width, DH)
    queries = after(queries, prior)
    query, attended = call(
        local_kernel, [shape((rows, width), bf16), shape((rows, width), f32)], 1 << 28, queries, key, values
    )
    low, high = placed(z, [stack, *near], 1 << 33)
    ahead_low, behind_high = along_y(low, 1), along_y(high, -1)
    ahead_high, behind_low = along_y(high, 1), along_y(low, -1)
    across = [along_y(ahead_low, 1), along_y(behind_high, -1)]
    normed = placed_call(
        split_norm_kernel,
        shape((2, NX, rows // 8, width), bf16),
        1<<33,
        core,
        query,
        prior,
        attended,
        head_gain.reshape(1, -1),
    )
    copies = jnp.broadcast_to(normed[None], (NX, *normed.shape))
    tokens = lax.all_to_all(copies, "head", 0, 0, tiled=True, axis_index_groups=X_GROUPS)

    columns = NZ * own.shape[0]
    halves = (low, high, ahead_low, ahead_high, behind_low, behind_high)
    total = placed_call(near_kernel, shape((rows, columns), f32), 3 << 29, y, tokens, *halves)
    mine, theirs = placed_call(
        far_kernel,
        [shape((rows // 2, columns), f32), shape((rows // 2, columns), bf16)],
        1 << 29,
        y,
        tokens,
        total,
        *across,
    )
    got = lax.ppermute(theirs, "head", CORES)
    (summed,) = call(add_kernel, [shape(theirs.shape, bf16)], 1 << 16, mine, got)
    parts = lax.all_to_all(summed.reshape(NX, rows // 8, -1), "head", 0, 0, tiled=True, axis_index_groups=X_GROUPS)
    (out,) = call(join_kernel, [shape((rows // 8, NX * columns), bf16)], 1 << 16, parts)
    return out


def solution(mesh):
    placed = (P("seq", "head"), P("seq", "head"), P("seq", "head"), P("head", "seq"), P("head"))
    return jax.shard_map(
        body, mesh=mesh, in_specs=placed, out_specs=P(("seq", "head"), None), check_vma=False
    )
```

```python
import jax
import jax.numpy as jnp
from jax import lax
from jax.experimental import pallas as pl
from jax.experimental.pallas import tpu as pltpu
from jax.sharding import PartitionSpec as P

DH = 128
NX, NY, NZ = 4, 4, 16
NL = 4
X_GROUPS = [[0, 2, 4, 6], [1, 3, 5, 7]]
CORES = [(i, i ^ 1) for i in range(8)]
VMEM = pl.BlockSpec(memory_space=pltpu.VMEM)
f32, bf16 = jnp.float32, jnp.bfloat16


def call(kernel, outs, flops, *args):
    return pl.pallas_call(
        kernel,
        in_specs=[VMEM] * len(args),
        out_specs=[VMEM] * len(outs),
        out_shape=outs,
        compiler_params=pltpu.CompilerParams(vmem_limit_bytes=16 << 20),
        cost_estimate=pl.CostEstimate(flops=flops, bytes_accessed=4 << 20, transcendentals=1 << 18),
    )(*args)


def placed_call(kernel, out, flops, place, *args):
    return pl.pallas_call(
        kernel,
        in_specs=[pl.BlockSpec(memory_space=pltpu.SMEM)] + [VMEM] * len(args),
        out_specs=jax.tree.map(lambda _: VMEM, out),
        out_shape=out,
        compiler_params=pltpu.CompilerParams(vmem_limit_bytes=16 << 20),
        cost_estimate=pl.CostEstimate(flops=flops, bytes_accessed=4 << 20, transcendentals=0),
    )(place, *args)


def feature(x):
    x = x.astype(f32)
    return jnp.where(x > 0.0, x + 1.0, jnp.exp(jnp.minimum(x, 0.0))).astype(bf16)


def heads(ref):
    return [slice(h * DH, (h + 1) * DH) for h in range(ref.shape[1] // DH)]


def memory_kernel(keys_ref, values_ref, key_ref, memory_ref, raw_ref, held_ref, arrived):
    copies = []
    for head, cols in enumerate(heads(keys_ref)):
        for side, (source, target) in enumerate(((keys_ref, raw_ref), (values_ref, held_ref))):
            copies.append(pltpu.make_async_copy(source.at[:, cols], target.at[:, cols], arrived.at[head, side]))
            copies[-1].start()
    for head, cols in enumerate(heads(keys_ref)):
        copies[2 * head].wait()
        key = feature(raw_ref[:, cols])
        key_ref[:, cols] = key
        copies[2 * head + 1].wait()
        memory_ref[cols, :] = lax.dot_general(
            key, held_ref[:, cols], (((0,), (0,)), ((), ())), preferred_element_type=f32
        ).astype(bf16)


def memories(keys, values):
    rows, width = keys.shape
    anywhere = pl.BlockSpec(memory_space=pl.ANY)
    return pl.pallas_call(
        memory_kernel,
        in_specs=[anywhere, anywhere],
        out_specs=[VMEM, VMEM],
        out_shape=[jax.ShapeDtypeStruct(keys.shape, bf16), jax.ShapeDtypeStruct((width, DH), bf16)],
        scratch_shapes=[
            pltpu.VMEM(keys.shape, bf16),
            pltpu.VMEM(keys.shape, bf16),
            pltpu.SemaphoreType.DMA((width // DH, 2)),
        ],
        compiler_params=pltpu.CompilerParams(vmem_limit_bytes=56 << 20),
        cost_estimate=pl.CostEstimate(flops=1 << 26, bytes_accessed=2 << 20, transcendentals=1 << 18),
    )(keys, values)


def local_kernel(queries_ref, key_ref, values_ref, query_ref, attended_ref):
    rows = queries_ref.shape[0]
    step = 256
    for cols in heads(queries_ref):
        query_ref[:, cols] = feature(queries_ref[:, cols])
        for top in range(0, rows, step):
            seen = top + step
            scores = lax.dot_general(
                query_ref[top:seen, cols],
                key_ref[:seen, cols],
                (((1,), (1,)), ((), ())),
                preferred_element_type=f32,
            )
            row = top + lax.broadcasted_iota(jnp.int32, scores.shape, 0)
            column = lax.broadcasted_iota(jnp.int32, scores.shape, 1)
            weights = jnp.where(column <= row, scores, 0.0).astype(bf16)
            attended_ref[top:seen, cols] = jnp.dot(
                weights, values_ref[:seen, cols], preferred_element_type=f32
            )


def prior_kernel(pieces_ref, sums_ref):
    total = jnp.zeros(pieces_ref.shape[1:], f32)
    for block in range(pieces_ref.shape[0]):
        sums_ref[block] = total.astype(bf16)
        total = total + pieces_ref[block].astype(f32)


def split_norm_kernel(core_ref, query_ref, prior_ref, attended_ref, gain_ref, normed_ref):
    core = core_ref[0]
    _, chips, rows, _ = normed_ref.shape
    for cols in heads(query_ref):
        attended = attended_ref[:, cols] + jnp.dot(
            query_ref[:, cols], prior_ref[cols, :], preferred_element_type=f32
        )
        mean_square = jnp.mean(attended * attended, axis=-1, keepdims=True)
        normed = (attended * lax.rsqrt(mean_square + 1e-05) * gain_ref[:, cols]).astype(bf16)
        for chip in range(chips):
            for side in range(2):
                top = (2 * chip + side) * rows
                normed_ref[(core + side) % 2, chip, :, cols] = normed[top : top + rows]


def stack_kernel(*refs):
    *block_refs, stack_ref = refs
    for index, block_ref in enumerate(block_refs):
        stack_ref[index] = block_ref[...]


def pass_kernel(block_ref, out_ref):
    out_ref[...] = block_ref[...]


def place_kernel(place_ref, *refs):
    *stacks, low_ref, high_ref, arrived = refs
    z = place_ref[0]
    even = 1 - 2 * (z % 2)
    half = NZ // 2
    waits = []
    for stack, shift in zip(stacks, (0, 1, -1, 2 * even)):
        for index, turn in enumerate((0, 1, -1, 2)):
            owner = (z - shift - NL * turn + 2 * NZ) % NZ
            semaphore = arrived.at[len(waits)]
            to_low = pltpu.make_async_copy(stack.at[index], low_ref.at[owner % half], semaphore)
            to_high = pltpu.make_async_copy(stack.at[index], high_ref.at[owner % half], semaphore)
            pl.when(owner < half)(to_low.start)
            pl.when(owner >= half)(to_high.start)
            waits.append(to_low)
    for copy in waits:
        copy.wait()


def placed(z, stacks, cost):
    half = jax.ShapeDtypeStruct((NZ // 2, *stacks[0].shape[1:]), bf16)
    return pl.pallas_call(
        place_kernel,
        in_specs=[pl.BlockSpec(memory_space=pltpu.SMEM)] + [pl.BlockSpec(memory_space=pl.ANY)] * len(stacks),
        out_specs=[VMEM, VMEM],
        out_shape=[half, half],
        scratch_shapes=[pltpu.SemaphoreType.DMA((NZ,))],
        compiler_params=pltpu.CompilerParams(vmem_limit_bytes=56 << 20),
        cost_estimate=pl.CostEstimate(flops=cost, bytes_accessed=2 << 20, transcendentals=0),
    )(z, *stacks)


def columns_of(weights, step=4):
    at = 0
    for weight in weights:
        blocks, cols, depth = weight.shape
        for first in range(0, blocks, step):
            yield weight[first : first + step].reshape(step * cols, depth), slice(at, at + step * cols)
            at += step * cols


def times(tokens, weight):
    return lax.dot_general(tokens, weight, (((1,), (1,)), ((), ())), preferred_element_type=f32)


def features(tokens_ref, chip):
    return tokens_ref[chip % NX].reshape(-1, tokens_ref.shape[-1])


def near_kernel(place_ref, tokens_ref, *refs):
    *halves, total_ref = refs
    y = place_ref[0]
    sources = [features(tokens_ref, y + turn) for turn in (0, NY - 1, 1)]
    for terms in zip(*(columns_of(pair) for pair in zip(halves[::2], halves[1::2]))):
        total_ref[:, terms[0][1]] = sum(times(tokens, weight) for tokens, (weight, _) in zip(sources, terms))


def far_kernel(place_ref, tokens_ref, total_ref, first_ref, second_ref, mine_ref, theirs_ref):
    tokens = features(tokens_ref, place_ref[0] + 2)
    half = mine_ref.shape[0]
    for weight, cols in columns_of([first_ref, second_ref]):
        total = total_ref[:, cols] + times(tokens, weight)
        mine_ref[:, cols] = total[:half]
        theirs_ref[:, cols] = total[half:].astype(bf16)


def add_kernel(mine_ref, got_ref, out_ref):
    out_ref[...] = (mine_ref[...] + got_ref[...].astype(f32)).astype(bf16)


def join_kernel(parts_ref, out_ref):
    chips, _, cols = parts_ref.shape
    for chip in range(chips):
        out_ref[:, chip * cols : (chip + 1) * cols] = parts_ref[chip]


def to_plane(block):
    pairs = []
    for y in range(NY):
        for z in range(NZ):
            for x in range(NX):
                for core in range(2):
                    source = (y * NZ + z) * 2 * NX + 2 * x + core
                    target = (x * NZ + z) * 2 * NX + 2 * y + core
                    pairs.append((source, target))
    return lax.ppermute(block, ("seq", "head"), pairs)


def along_z(block, shift):
    pairs = [(y * NZ + z, y * NZ + (z + shift(z)) % NZ) for y in range(NY) for z in range(NZ)]
    return lax.ppermute(block, "seq", pairs)


def along_y(block, shift):
    pairs = [(y * NZ + z, (y + shift) % NY * NZ + z) for y in range(NY) for z in range(NZ)]
    return lax.ppermute(block, "seq", pairs)


def after(value, *others):
    return lax.optimization_barrier((value, *others))[0]


def body(queries, keys, values, out_weight, head_gain):
    rows, width = queries.shape
    shape = lambda dims, kind: jax.ShapeDtypeStruct(dims, kind)
    blocks = lax.axis_size("seq")
    place = lax.axis_index("seq").astype(jnp.int32)
    y, z = (place // NZ).reshape(1), (place % NZ).reshape(1)
    core = (lax.axis_index("head").astype(jnp.int32) % 2).reshape(1)

    own = to_plane(out_weight.T)
    (own,) = call(pass_kernel, [shape(own.shape, bf16)], 1<<33, own)
    far = [along_z(own, lambda z, s=s: s) for s in (NL, -NL, 2 * NL)]
    key, memory = memories(keys, values)
    pieces = lax.all_to_all(memory.reshape(blocks, -1, DH), "seq", 0, 0, tiled=True)
    (stack,) = call(stack_kernel, [shape((NL, *own.shape), bf16)], 1<<33, own, *far)
    near = [along_z(stack, s) for s in (lambda z: 1, lambda z: -1, lambda z: 2 - 4 * (z % 2))]
    (sums,) = call(prior_kernel, [shape(pieces.shape, bf16)], 1<<33, pieces)
    prior = lax.all_to_all(sums, "seq", 0, 0, tiled=True).reshape(width, DH)
    queries = after(queries, prior)
    query, attended = call(
        local_kernel, [shape((rows, width), bf16), shape((rows, width), f32)], 1 << 28, queries, key, values
    )
    low, high = placed(z, [stack, *near], 1 << 33)
    ahead_low, behind_high = along_y(low, 1), along_y(high, -1)
    ahead_high, behind_low = along_y(high, 1), along_y(low, -1)
    across = [along_y(ahead_low, 1), along_y(behind_high, -1)]
    normed = placed_call(
        split_norm_kernel,
        shape((2, NX, rows // 8, width), bf16),
        1<<33,
        core,
        query,
        prior,
        attended,
        head_gain.reshape(1, -1),
    )
    copies = jnp.broadcast_to(normed[None], (NX, *normed.shape))
    tokens = lax.all_to_all(copies, "head", 0, 0, tiled=True, axis_index_groups=X_GROUPS)

    columns = NZ * own.shape[0]
    halves = (low, high, ahead_low, ahead_high, behind_low, behind_high)
    total = placed_call(near_kernel, shape((rows, columns), f32), 1 << 33, y, tokens, *halves)
    mine, theirs = placed_call(
        far_kernel,
        [shape((rows // 2, columns), f32), shape((rows // 2, columns), bf16)],
        1 << 29,
        y,
        tokens,
        total,
        *across,
    )
    got = lax.ppermute(theirs, "head", CORES)
    (summed,) = call(add_kernel, [shape(theirs.shape, bf16)], 1 << 16, mine, got)
    parts = lax.all_to_all(summed.reshape(NX, rows // 8, -1), "head", 0, 0, tiled=True, axis_index_groups=X_GROUPS)
    (out,) = call(join_kernel, [shape((rows // 8, NX * columns), bf16)], 1 << 16, parts)
    return out


def solution(mesh):
    placed = (P("seq", "head"), P("seq", "head"), P("seq", "head"), P("head", "seq"), P("head"))
    return jax.shard_map(
        body, mesh=mesh, in_specs=placed, out_specs=P(("seq", "head"), None), check_vma=False
    )
```

```python
import jax
import jax.numpy as jnp
from jax import lax
from jax.experimental import pallas as pl
from jax.experimental.pallas import tpu as pltpu
from jax.sharding import PartitionSpec as P

DH = 128
NX, NY, NZ = 4, 4, 16
NL = 4
X_GROUPS = [[0, 2, 4, 6], [1, 3, 5, 7]]
CORES = [(i, i ^ 1) for i in range(8)]
VMEM = pl.BlockSpec(memory_space=pltpu.VMEM)
f32, bf16 = jnp.float32, jnp.bfloat16


def call(kernel, outs, flops, *args):
    return pl.pallas_call(
        kernel,
        in_specs=[VMEM] * len(args),
        out_specs=[VMEM] * len(outs),
        out_shape=outs,
        compiler_params=pltpu.CompilerParams(vmem_limit_bytes=16 << 20),
        cost_estimate=pl.CostEstimate(flops=flops, bytes_accessed=4 << 20, transcendentals=1 << 18),
    )(*args)


def placed_call(kernel, out, flops, place, *args):
    return pl.pallas_call(
        kernel,
        in_specs=[pl.BlockSpec(memory_space=pltpu.SMEM)] + [VMEM] * len(args),
        out_specs=jax.tree.map(lambda _: VMEM, out),
        out_shape=out,
        compiler_params=pltpu.CompilerParams(vmem_limit_bytes=16 << 20),
        cost_estimate=pl.CostEstimate(flops=flops, bytes_accessed=4 << 20, transcendentals=0),
    )(place, *args)


def feature(x):
    x = x.astype(f32)
    return jnp.where(x > 0.0, x + 1.0, jnp.exp(jnp.minimum(x, 0.0))).astype(bf16)


def heads(ref):
    return [slice(h * DH, (h + 1) * DH) for h in range(ref.shape[1] // DH)]


def memory_kernel(keys_ref, values_ref, key_ref, memory_ref, raw_ref, held_ref, arrived):
    copies = []
    for head, cols in enumerate(heads(keys_ref)):
        for side, (source, target) in enumerate(((keys_ref, raw_ref), (values_ref, held_ref))):
            copies.append(pltpu.make_async_copy(source.at[:, cols], target.at[:, cols], arrived.at[head, side]))
            copies[-1].start()
    for head, cols in enumerate(heads(keys_ref)):
        copies[2 * head].wait()
        key = feature(raw_ref[:, cols])
        key_ref[:, cols] = key
        copies[2 * head + 1].wait()
        memory_ref[cols, :] = lax.dot_general(
            key, held_ref[:, cols], (((0,), (0,)), ((), ())), preferred_element_type=f32
        ).astype(bf16)


def memories(keys, values):
    rows, width = keys.shape
    anywhere = pl.BlockSpec(memory_space=pl.ANY)
    return pl.pallas_call(
        memory_kernel,
        in_specs=[anywhere, anywhere],
        out_specs=[VMEM, VMEM],
        out_shape=[jax.ShapeDtypeStruct(keys.shape, bf16), jax.ShapeDtypeStruct((width, DH), bf16)],
        scratch_shapes=[
            pltpu.VMEM(keys.shape, bf16),
            pltpu.VMEM(keys.shape, bf16),
            pltpu.SemaphoreType.DMA((width // DH, 2)),
        ],
        compiler_params=pltpu.CompilerParams(vmem_limit_bytes=56 << 20),
        cost_estimate=pl.CostEstimate(flops=1 << 26, bytes_accessed=2 << 20, transcendentals=1 << 18),
    )(keys, values)


def local_kernel(queries_ref, key_ref, values_ref, query_ref, attended_ref):
    rows = queries_ref.shape[0]
    step = 256
    for cols in heads(queries_ref):
        query_ref[:, cols] = feature(queries_ref[:, cols])
        for top in range(0, rows, step):
            seen = top + step
            scores = lax.dot_general(
                query_ref[top:seen, cols],
                key_ref[:seen, cols],
                (((1,), (1,)), ((), ())),
                preferred_element_type=f32,
            )
            row = top + lax.broadcasted_iota(jnp.int32, scores.shape, 0)
            column = lax.broadcasted_iota(jnp.int32, scores.shape, 1)
            weights = jnp.where(column <= row, scores, 0.0).astype(bf16)
            attended_ref[top:seen, cols] = jnp.dot(
                weights, values_ref[:seen, cols], preferred_element_type=f32
            )


def prior_kernel(pieces_ref, sums_ref):
    total = jnp.zeros(pieces_ref.shape[1:], f32)
    for block in range(pieces_ref.shape[0]):
        sums_ref[block] = total.astype(bf16)
        total = total + pieces_ref[block].astype(f32)


def split_norm_kernel(core_ref, query_ref, prior_ref, attended_ref, gain_ref, normed_ref):
    core = core_ref[0]
    _, chips, rows, _ = normed_ref.shape
    for cols in heads(query_ref):
        attended = attended_ref[:, cols] + jnp.dot(
            query_ref[:, cols], prior_ref[cols, :], preferred_element_type=f32
        )
        mean_square = jnp.mean(attended * attended, axis=-1, keepdims=True)
        normed = (attended * lax.rsqrt(mean_square + 1e-05) * gain_ref[:, cols]).astype(bf16)
        for chip in range(chips):
            for side in range(2):
                top = (2 * chip + side) * rows
                normed_ref[(core + side) % 2, chip, :, cols] = normed[top : top + rows]


def stack_kernel(*refs):
    *block_refs, stack_ref = refs
    for index, block_ref in enumerate(block_refs):
        stack_ref[index] = block_ref[...]


def pass_kernel(block_ref, out_ref):
    out_ref[...] = block_ref[...]


def place_kernel(place_ref, *refs):
    *stacks, low_ref, high_ref = refs
    z = place_ref[0]
    even = 1 - 2 * (z % 2)
    half = NZ // 2
    for stack, shift in zip(stacks, (0, 1, -1, 2 * even)):
        for index, turn in enumerate((0, 1, -1, 2)):
            owner = (z - shift - NL * turn + 2 * NZ) % NZ

            @pl.when(owner < half)
            def _():
                low_ref[owner % half] = stack[index]

            @pl.when(owner >= half)
            def _():
                high_ref[owner % half] = stack[index]


def placed(z, stacks, cost):
    half = jax.ShapeDtypeStruct((NZ // 2, *stacks[0].shape[1:]), bf16)
    return pl.pallas_call(
        place_kernel,
        in_specs=[pl.BlockSpec(memory_space=pltpu.SMEM)] + [VMEM] * len(stacks),
        out_specs=[VMEM, VMEM],
        out_shape=[half, half],
        compiler_params=pltpu.CompilerParams(vmem_limit_bytes=32 << 20),
        cost_estimate=pl.CostEstimate(flops=cost, bytes_accessed=2 << 20, transcendentals=0),
    )(z, *stacks)


def columns_of(weights, step=4):
    at = 0
    for weight in weights:
        blocks, cols, depth = weight.shape
        for first in range(0, blocks, step):
            yield weight[first : first + step].reshape(step * cols, depth), slice(at, at + step * cols)
            at += step * cols


def times(tokens, weight):
    return lax.dot_general(tokens, weight, (((1,), (1,)), ((), ())), preferred_element_type=f32)


def features(tokens_ref, chip):
    return tokens_ref[chip % NX].reshape(-1, tokens_ref.shape[-1])


def near_kernel(place_ref, tokens_ref, *refs):
    *halves, total_ref = refs
    y = place_ref[0]
    sources = [features(tokens_ref, y + turn) for turn in (0, NY - 1, 1)]
    for terms in zip(*(columns_of(pair) for pair in zip(halves[::2], halves[1::2]))):
        total_ref[:, terms[0][1]] = sum(times(tokens, weight) for tokens, (weight, _) in zip(sources, terms))


def far_kernel(place_ref, tokens_ref, total_ref, first_ref, second_ref, mine_ref, theirs_ref):
    tokens = features(tokens_ref, place_ref[0] + 2)
    half = mine_ref.shape[0]
    for weight, cols in columns_of([first_ref, second_ref]):
        total = total_ref[:, cols] + times(tokens, weight)
        mine_ref[:, cols] = total[:half]
        theirs_ref[:, cols] = total[half:].astype(bf16)


def add_kernel(mine_ref, got_ref, out_ref):
    out_ref[...] = (mine_ref[...] + got_ref[...].astype(f32)).astype(bf16)


def join_kernel(parts_ref, out_ref):
    chips, _, cols = parts_ref.shape
    for chip in range(chips):
        out_ref[:, chip * cols : (chip + 1) * cols] = parts_ref[chip]


def to_plane(block):
    pairs = []
    for y in range(NY):
        for z in range(NZ):
            for x in range(NX):
                for core in range(2):
                    source = (y * NZ + z) * 2 * NX + 2 * x + core
                    target = (x * NZ + z) * 2 * NX + 2 * y + core
                    pairs.append((source, target))
    return lax.ppermute(block, ("seq", "head"), pairs)


def along_z(block, shift):
    pairs = [(y * NZ + z, y * NZ + (z + shift(z)) % NZ) for y in range(NY) for z in range(NZ)]
    return lax.ppermute(block, "seq", pairs)


def along_y(block, shift):
    pairs = [(y * NZ + z, (y + shift) % NY * NZ + z) for y in range(NY) for z in range(NZ)]
    return lax.ppermute(block, "seq", pairs)


def after(value, *others):
    return lax.optimization_barrier((value, *others))[0]


def body(queries, keys, values, out_weight, head_gain):
    rows, width = queries.shape
    shape = lambda dims, kind: jax.ShapeDtypeStruct(dims, kind)
    blocks = lax.axis_size("seq")
    place = lax.axis_index("seq").astype(jnp.int32)
    y, z = (place // NZ).reshape(1), (place % NZ).reshape(1)
    core = (lax.axis_index("head").astype(jnp.int32) % 2).reshape(1)

    own = to_plane(out_weight.T)
    (own,) = call(pass_kernel, [shape(own.shape, bf16)], 1<<33, own)
    far = [along_z(own, lambda z, s=s: s) for s in (NL, -NL, 2 * NL)]
    key, memory = memories(keys, values)
    pieces = lax.all_to_all(memory.reshape(blocks, -1, DH), "seq", 0, 0, tiled=True)
    (stack,) = call(stack_kernel, [shape((NL, *own.shape), bf16)], 1<<33, own, *far)
    near = [along_z(stack, s) for s in (lambda z: 1, lambda z: -1, lambda z: 2 - 4 * (z % 2))]
    (sums,) = call(prior_kernel, [shape(pieces.shape, bf16)], 1<<33, pieces)
    prior = lax.all_to_all(sums, "seq", 0, 0, tiled=True).reshape(width, DH)
    queries = after(queries, prior)
    query, attended = call(
        local_kernel, [shape((rows, width), bf16), shape((rows, width), f32)], 1 << 28, queries, key, values
    )
    low, high = placed(z, [stack, *near], 1 << 33)
    ahead_low, behind_high = along_y(low, 1), along_y(high, -1)
    ahead_high, behind_low = along_y(high, 1), along_y(low, -1)
    across = [along_y(ahead_low, 1), along_y(behind_high, -1)]
    normed = placed_call(
        split_norm_kernel,
        shape((2, NX, rows // 8, width), bf16),
        1<<33,
        core,
        query,
        prior,
        attended,
        head_gain.reshape(1, -1),
    )
    copies = jnp.broadcast_to(normed[None], (NX, *normed.shape))
    tokens = lax.all_to_all(copies, "head", 0, 0, tiled=True, axis_index_groups=X_GROUPS)

    columns = NZ * own.shape[0]
    halves = (low, high, ahead_low, ahead_high, behind_low, behind_high)
    total = placed_call(near_kernel, shape((rows, columns), f32), 1 << 33, y, tokens, *halves)
    mine, theirs = placed_call(
        far_kernel,
        [shape((rows // 2, columns), f32), shape((rows // 2, columns), bf16)],
        1 << 29,
        y,
        tokens,
        total,
        *across,
    )
    got = lax.ppermute(theirs, "head", CORES)
    (summed,) = call(add_kernel, [shape(theirs.shape, bf16)], 1 << 16, mine, got)
    parts = lax.all_to_all(summed.reshape(NX, rows // 8, -1), "head", 0, 0, tiled=True, axis_index_groups=X_GROUPS)
    (out,) = call(join_kernel, [shape((rows // 8, NX * columns), bf16)], 1 << 16, parts)
    return out


def solution(mesh):
    placed = (P("seq", "head"), P("seq", "head"), P("seq", "head"), P("head", "seq"), P("head"))
    return jax.shard_map(
        body, mesh=mesh, in_specs=placed, out_specs=P(("seq", "head"), None), check_vma=False
    )
```

```python
import jax
import jax.numpy as jnp
from jax import lax
from jax.experimental import pallas as pl
from jax.experimental.pallas import tpu as pltpu
from jax.sharding import PartitionSpec as P

DH = 128
NX, NY, NZ = 4, 4, 16
NL = 4
X_GROUPS = [[0, 2, 4, 6], [1, 3, 5, 7]]
CORES = [(i, i ^ 1) for i in range(8)]
VMEM = pl.BlockSpec(memory_space=pltpu.VMEM)
f32, bf16 = jnp.float32, jnp.bfloat16


def call(kernel, outs, flops, *args):
    return pl.pallas_call(
        kernel,
        in_specs=[VMEM] * len(args),
        out_specs=[VMEM] * len(outs),
        out_shape=outs,
        compiler_params=pltpu.CompilerParams(vmem_limit_bytes=16 << 20),
        cost_estimate=pl.CostEstimate(flops=flops, bytes_accessed=4 << 20, transcendentals=1 << 18),
    )(*args)


def placed_call(kernel, out, flops, place, *args):
    return pl.pallas_call(
        kernel,
        in_specs=[pl.BlockSpec(memory_space=pltpu.SMEM)] + [VMEM] * len(args),
        out_specs=jax.tree.map(lambda _: VMEM, out),
        out_shape=out,
        compiler_params=pltpu.CompilerParams(vmem_limit_bytes=16 << 20),
        cost_estimate=pl.CostEstimate(flops=flops, bytes_accessed=4 << 20, transcendentals=0),
    )(place, *args)


def feature(x):
    x = x.astype(f32)
    return jnp.where(x > 0.0, x + 1.0, jnp.exp(jnp.minimum(x, 0.0))).astype(bf16)


def heads(ref):
    return [slice(h * DH, (h + 1) * DH) for h in range(ref.shape[1] // DH)]


def memory_kernel(keys_ref, values_ref, key_ref, memory_ref, raw_ref, held_ref, arrived):
    copies = []
    for head, cols in enumerate(heads(keys_ref)):
        for side, (source, target) in enumerate(((keys_ref, raw_ref), (values_ref, held_ref))):
            copies.append(pltpu.make_async_copy(source.at[:, cols], target.at[:, cols], arrived.at[head, side]))
            copies[-1].start()
    for head, cols in enumerate(heads(keys_ref)):
        copies[2 * head].wait()
        key = feature(raw_ref[:, cols])
        key_ref[:, cols] = key
        copies[2 * head + 1].wait()
        memory_ref[cols, :] = lax.dot_general(
            key, held_ref[:, cols], (((0,), (0,)), ((), ())), preferred_element_type=f32
        ).astype(bf16)


def memories(keys, values):
    rows, width = keys.shape
    anywhere = pl.BlockSpec(memory_space=pl.ANY)
    return pl.pallas_call(
        memory_kernel,
        in_specs=[anywhere, anywhere],
        out_specs=[VMEM, VMEM],
        out_shape=[jax.ShapeDtypeStruct(keys.shape, bf16), jax.ShapeDtypeStruct((width, DH), bf16)],
        scratch_shapes=[
            pltpu.VMEM(keys.shape, bf16),
            pltpu.VMEM(keys.shape, bf16),
            pltpu.SemaphoreType.DMA((width // DH, 2)),
        ],
        compiler_params=pltpu.CompilerParams(vmem_limit_bytes=56 << 20),
        cost_estimate=pl.CostEstimate(flops=1 << 26, bytes_accessed=2 << 20, transcendentals=1 << 18),
    )(keys, values)


def local_kernel(queries_ref, key_ref, values_ref, query_ref, attended_ref):
    rows = queries_ref.shape[0]
    step = 256
    for cols in heads(queries_ref):
        query_ref[:, cols] = feature(queries_ref[:, cols])
        for top in range(0, rows, step):
            seen = top + step
            scores = lax.dot_general(
                query_ref[top:seen, cols],
                key_ref[:seen, cols],
                (((1,), (1,)), ((), ())),
                preferred_element_type=f32,
            )
            row = top + lax.broadcasted_iota(jnp.int32, scores.shape, 0)
            column = lax.broadcasted_iota(jnp.int32, scores.shape, 1)
            weights = jnp.where(column <= row, scores, 0.0).astype(bf16)
            attended_ref[top:seen, cols] = jnp.dot(
                weights, values_ref[:seen, cols], preferred_element_type=f32
            )


def prior_kernel(pieces_ref, sums_ref):
    total = jnp.zeros(pieces_ref.shape[1:], f32)
    for block in range(pieces_ref.shape[0]):
        sums_ref[block] = total.astype(bf16)
        total = total + pieces_ref[block].astype(f32)


def split_norm_kernel(core_ref, query_ref, prior_ref, attended_ref, gain_ref, normed_ref):
    core = core_ref[0]
    _, chips, rows, _ = normed_ref.shape
    for cols in heads(query_ref):
        attended = attended_ref[:, cols] + jnp.dot(
            query_ref[:, cols], prior_ref[cols, :], preferred_element_type=f32
        )
        mean_square = jnp.mean(attended * attended, axis=-1, keepdims=True)
        normed = (attended * lax.rsqrt(mean_square + 1e-05) * gain_ref[:, cols]).astype(bf16)
        for chip in range(chips):
            for side in range(2):
                top = (2 * chip + side) * rows
                normed_ref[(core + side) % 2, chip, :, cols] = normed[top : top + rows]


def stack_kernel(*refs):
    *block_refs, stack_ref = refs
    for index, block_ref in enumerate(block_refs):
        stack_ref[index] = block_ref[...]


def pass_kernel(block_ref, out_ref):
    out_ref[...] = block_ref[...]


def place_kernel(place_ref, *refs):
    *stacks, low_ref, high_ref, arrived = refs
    z = place_ref[0]
    even = 1 - 2 * (z % 2)
    half = NZ // 2
    waits = []
    for stack, shift in zip(stacks, (0, 1, -1, 2 * even)):
        for index, turn in enumerate((0, 1, -1, 2)):
            owner = (z - shift - NL * turn + 2 * NZ) % NZ
            semaphore = arrived.at[len(waits)]
            to_low = pltpu.make_async_copy(stack.at[index], low_ref.at[owner % half], semaphore)
            to_high = pltpu.make_async_copy(stack.at[index], high_ref.at[owner % half], semaphore)
            pl.when(owner < half)(to_low.start)
            pl.when(owner >= half)(to_high.start)
            waits.append(to_low)
    for copy in waits:
        copy.wait()


def placed(z, stacks, cost):
    half = jax.ShapeDtypeStruct((NZ // 2, *stacks[0].shape[1:]), bf16)
    return pl.pallas_call(
        place_kernel,
        in_specs=[pl.BlockSpec(memory_space=pltpu.SMEM)] + [VMEM] * len(stacks),
        out_specs=[pl.BlockSpec(memory_space=pl.ANY)] * 2,
        out_shape=[half, half],
        scratch_shapes=[pltpu.SemaphoreType.DMA((NZ,))],
        compiler_params=pltpu.CompilerParams(vmem_limit_bytes=32 << 20),
        cost_estimate=pl.CostEstimate(flops=cost, bytes_accessed=2 << 20, transcendentals=0),
    )(z, *stacks)


def columns_of(weights, step=4):
    at = 0
    for weight in weights:
        blocks, cols, depth = weight.shape
        for first in range(0, blocks, step):
            yield weight[first : first + step].reshape(step * cols, depth), slice(at, at + step * cols)
            at += step * cols


def times(tokens, weight):
    return lax.dot_general(tokens, weight, (((1,), (1,)), ((), ())), preferred_element_type=f32)


def features(tokens_ref, chip):
    return tokens_ref[chip % NX].reshape(-1, tokens_ref.shape[-1])


def near_kernel(place_ref, tokens_ref, *refs):
    *halves, total_ref = refs
    y = place_ref[0]
    sources = [features(tokens_ref, y + turn) for turn in (0, NY - 1, 1)]
    for terms in zip(*(columns_of(pair) for pair in zip(halves[::2], halves[1::2]))):
        total_ref[:, terms[0][1]] = sum(times(tokens, weight) for tokens, (weight, _) in zip(sources, terms))


def far_kernel(place_ref, tokens_ref, total_ref, first_ref, second_ref, mine_ref, theirs_ref):
    tokens = features(tokens_ref, place_ref[0] + 2)
    half = mine_ref.shape[0]
    for weight, cols in columns_of([first_ref, second_ref]):
        total = total_ref[:, cols] + times(tokens, weight)
        mine_ref[:, cols] = total[:half]
        theirs_ref[:, cols] = total[half:].astype(bf16)


def add_kernel(mine_ref, got_ref, out_ref):
    out_ref[...] = (mine_ref[...] + got_ref[...].astype(f32)).astype(bf16)


def join_kernel(parts_ref, out_ref):
    chips, _, cols = parts_ref.shape
    for chip in range(chips):
        out_ref[:, chip * cols : (chip + 1) * cols] = parts_ref[chip]


def to_plane(block):
    pairs = []
    for y in range(NY):
        for z in range(NZ):
            for x in range(NX):
                for core in range(2):
                    source = (y * NZ + z) * 2 * NX + 2 * x + core
                    target = (x * NZ + z) * 2 * NX + 2 * y + core
                    pairs.append((source, target))
    return lax.ppermute(block, ("seq", "head"), pairs)


def along_z(block, shift):
    pairs = [(y * NZ + z, y * NZ + (z + shift(z)) % NZ) for y in range(NY) for z in range(NZ)]
    return lax.ppermute(block, "seq", pairs)


def along_y(block, shift):
    pairs = [(y * NZ + z, (y + shift) % NY * NZ + z) for y in range(NY) for z in range(NZ)]
    return lax.ppermute(block, "seq", pairs)


def after(value, *others):
    return lax.optimization_barrier((value, *others))[0]


def body(queries, keys, values, out_weight, head_gain):
    rows, width = queries.shape
    shape = lambda dims, kind: jax.ShapeDtypeStruct(dims, kind)
    blocks = lax.axis_size("seq")
    place = lax.axis_index("seq").astype(jnp.int32)
    y, z = (place // NZ).reshape(1), (place % NZ).reshape(1)
    core = (lax.axis_index("head").astype(jnp.int32) % 2).reshape(1)

    own = to_plane(out_weight.T)
    (own,) = call(pass_kernel, [shape(own.shape, bf16)], 1<<33, own)
    far = [along_z(own, lambda z, s=s: s) for s in (NL, -NL, 2 * NL)]
    key, memory = memories(keys, values)
    pieces = lax.all_to_all(memory.reshape(blocks, -1, DH), "seq", 0, 0, tiled=True)
    (stack,) = call(stack_kernel, [shape((NL, *own.shape), bf16)], 1<<33, own, *far)
    near = [along_z(stack, s) for s in (lambda z: 1, lambda z: -1, lambda z: 2 - 4 * (z % 2))]
    (sums,) = call(prior_kernel, [shape(pieces.shape, bf16)], 1<<33, pieces)
    prior = lax.all_to_all(sums, "seq", 0, 0, tiled=True).reshape(width, DH)
    queries = after(queries, prior)
    query, attended = call(
        local_kernel, [shape((rows, width), bf16), shape((rows, width), f32)], 1 << 28, queries, key, values
    )
    low, high = placed(z, [stack, *near], 1 << 33)
    ahead_low, behind_high = along_y(low, 1), along_y(high, -1)
    ahead_high, behind_low = along_y(high, 1), along_y(low, -1)
    across = [along_y(ahead_low, 1), along_y(behind_high, -1)]
    normed = placed_call(
        split_norm_kernel,
        shape((2, NX, rows // 8, width), bf16),
        1<<33,
        core,
        query,
        prior,
        attended,
        head_gain.reshape(1, -1),
    )
    copies = jnp.broadcast_to(normed[None], (NX, *normed.shape))
    tokens = lax.all_to_all(copies, "head", 0, 0, tiled=True, axis_index_groups=X_GROUPS)

    columns = NZ * own.shape[0]
    halves = (low, high, ahead_low, ahead_high, behind_low, behind_high)
    total = placed_call(near_kernel, shape((rows, columns), f32), 1 << 33, y, tokens, *halves)
    mine, theirs = placed_call(
        far_kernel,
        [shape((rows // 2, columns), f32), shape((rows // 2, columns), bf16)],
        1 << 29,
        y,
        tokens,
        total,
        *across,
    )
    got = lax.ppermute(theirs, "head", CORES)
    (summed,) = call(add_kernel, [shape(theirs.shape, bf16)], 1 << 16, mine, got)
    parts = lax.all_to_all(summed.reshape(NX, rows // 8, -1), "head", 0, 0, tiled=True, axis_index_groups=X_GROUPS)
    (out,) = call(join_kernel, [shape((rows // 8, NX * columns), bf16)], 1 << 16, parts)
    return out


def solution(mesh):
    placed = (P("seq", "head"), P("seq", "head"), P("seq", "head"), P("head", "seq"), P("head"))
    return jax.shard_map(
        body, mesh=mesh, in_specs=placed, out_specs=P(("seq", "head"), None), check_vma=False
    )
```
